32 devices in a mesh: wide: 4 (over z), narrow: 8 (over y, x, core).
Axes of the slice: x: 2, y: 2, z: 4, core: 2. Of those that a mesh axis runs over, the one named last changes fastest.
Arguments:
- matrix: bfloat16 [6144, 16384], P('narrow', 'wide'), as said below
- pivots: int32 [256], replicated, may hold values from 256 to 6143, as said below
Outputs:
- factored: bfloat16 [6144, 16384], P('narrow', 'wide')
The draws below stay inside these ranges and needn't reach their ends.
Inputs may be any that keep to these rules, and one draw needn't show every extreme that they name: `pivots`: distinct global row numbers below the panel; both 256 and 6143 occur. `matrix`: the first 256 stored columns hold a factored panel whose entries are smaller than the rest by about the square root of 256.
All inputs are finite; a program needn't handle non-finite values.
Results may differ from the reference program's by a relative error of at most 0.0048.
Values may be sent and summed in bfloat16 or wider, within the bound.
A program may use at most 64 MiB of HBM per device.

```python
import jax
import jax.numpy as jnp
from jax import lax

PANEL = 256
ROWS_DEV = 768
ORDER = 16384
ROWS = 6144
N_NARROW = 8


def draw_matrix(key, part):
    key = jax.random.fold_in(key, 11)
    first = jax.random.fold_in(key, 0)
    values = jnp.clip(jax.random.normal(first, (ROWS, ORDER), jnp.float32), -6.0, 6.0)
    column = jax.lax.broadcasted_iota(jnp.int32, (1, ORDER), 1)
    factor = jnp.where(column < PANEL, PANEL ** (-0.5), 1.0).astype(jnp.float32)
    return (values * factor).astype(jnp.bfloat16)


def draw_pivots(key, part):
    key = jax.random.fold_in(key, 23)
    first, second = jax.random.split(key)
    inner = jax.random.permutation(first, ROWS - PANEL - 2)[:PANEL - 2] + PANEL + 1
    values = jnp.concatenate([jnp.array([PANEL, ROWS - 1], jnp.int32), inner.astype(jnp.int32)])
    order = jax.random.permutation(second, PANEL)
    return values[order].astype(jnp.int32)


def setup_inputs(seed: int = 0) -> dict:
    keys = jax.random.split(jax.random.key(seed), 3)
    matrix = draw_matrix(jax.random.fold_in(keys[2], 71), 0)
    pivots = draw_pivots(jax.random.fold_in(keys[2], 71), 0)
    return {"matrix": matrix, "pivots": pivots}


def stored_rows(pivots):
    blocks = pivots // PANEL
    return (blocks % N_NARROW * ROWS_DEV + blocks // N_NARROW * PANEL + pivots % PANEL).astype(jnp.int32)

def reference(matrix, pivots):
    panel = matrix[:, :PANEL]
    rest = matrix[:, PANEL:]
    targets = stored_rows(pivots)
    pivot_rows = rest[targets]
    rest = rest.at[targets].set(rest[:PANEL])
    unit_lower = jnp.tril(panel[:PANEL].astype(jnp.float32), -1) + jnp.eye(PANEL, dtype=jnp.float32)
    upper = jax.scipy.linalg.solve_triangular(unit_lower, pivot_rows.astype(jnp.float32), lower=True, unit_diagonal=True).astype(jnp.bfloat16)
    columns = rest.shape[1]
    below = rest[PANEL:].reshape(-1, PANEL, columns)
    factors = panel[PANEL:].reshape(-1, PANEL, PANEL)

    def update(pair):
        block, left = pair
        return (block.astype(jnp.float32) - jnp.dot(left.astype(jnp.float32), upper.astype(jnp.float32), preferred_element_type=jnp.float32)).astype(jnp.bfloat16)
    lowered = lax.map(update, (below, factors)).reshape(-1, columns)
    return jnp.concatenate([panel, jnp.concatenate([upper, lowered], axis=0)], axis=1)
```

```python
import functools

import jax
import jax.numpy as jnp
from jax import lax
from jax.experimental import pallas as pl
from jax.experimental.pallas import tpu as pltpu
from jax.sharding import PartitionSpec as P

MESH = pl.DeviceIdType.MESH
CHUNKS = 8


def local_targets(pivots, width, narrow_count, narrow_pos):
    blocks = jnp.right_shift(pivots, width.bit_length() - 1)
    owner = jnp.bitwise_and(blocks, narrow_count - 1)
    inner = jnp.right_shift(blocks, narrow_count.bit_length() - 1)
    rows = inner * width + jnp.bitwise_and(pivots, width - 1)
    return jnp.where(owner == narrow_pos, rows, -1)


def exchange(
    narrow_count,
    wide_count,
    pivots,
    matrix,
    upper,
    top,
    panel,
    slices,
    pick,
    outgoing,
    held,
    arrived,
    partial,
    lower,
    inverse,
    solved,
    load_sem,
    local_sem,
    pair_sems,
    halve_sems,
    gather_sems,
    share_sems,
    chain_sems,
    near_sems,
    panel_sems,
    lower_sems,
):
    n = narrow_count
    bits = n.bit_length() - 1
    half = n // 2
    chips = half
    rows_dev, cols = matrix.shape
    width = pick.shape[0]
    cut = cols // n
    z = lax.axis_index("wide")
    me = lax.axis_index("narrow")
    core = me % 2
    chip = me // 2
    mate = me + 1 - 2 * core
    value = [(me // 2**q) % 2 for q in range(bits)]
    flip = [me + (1 - 2 * value[q]) * 2**q for q in range(bits)]

    def by_core(side, first, second):
        return first * (1 - side) + second * side

    def slice_of(r, side):
        total = side
        for q in range(1, bits):
            f0 = (r // 2 ** (bits - 1 - q)) % 2
            f1 = (r // 2 ** (q - 1)) % 2
            f = by_core(side, f0, f1)
            total = total + (value[q] + f * (1 - 2 * value[q])) * 2**q
        return total

    def partner(k):
        return by_core(core, flip[1 + k], flip[bits - 1 - k])

    def remote(src, dst, sems, i, to):
        return pltpu.make_async_remote_copy(
            src_ref=src,
            dst_ref=dst,
            send_sem=sems.at[0, i],
            recv_sem=sems.at[1, i],
            device_id=to,
            device_id_type=MESH,
        )

    ring = 0
    for q in range(1, bits):
        ring = ring + (sum(value[q:]) % 2) * 2 ** (q - 1)
    order = by_core(core, ring, (chips - ring) % chips)
    following = (ring + 1 - 2 * core + chips) % chips
    chip_next = 0
    for q in range(bits - 1):
        low = (following // 2**q) % 2
        high = (following // 2 ** (q + 1)) % 2
        chip_next = chip_next + ((low + high) % 2) * 2**q
    chain_to = chip_next * 2 + core
    chunk = width // 2 // CHUNKS
    root = me == 0
    has_next = order < chips - 1

    def load(j):
        return pltpu.make_async_copy(
            matrix.at[:, pl.ds(pl.multiple_of(j * cut, cut), cut)],
            slices.at[j],
            load_sem.at[j],
        )

    for j in range(n):
        load(j).start()

    barrier = pltpu.get_barrier_semaphore()
    for q in range(bits):
        pl.semaphore_signal(barrier, inc=1, device_id=(z, flip[q]), device_id_type=MESH)

    @pl.when(z > 0)
    def _():
        pl.semaphore_signal(barrier, inc=1, device_id=(z - 1, me), device_id_type=MESH)

    @pl.when(z < wide_count - 1)
    def _():
        pl.semaphore_signal(barrier, inc=1, device_id=(z + 1, me), device_id_type=MESH)

    target = local_targets(pivots[...], width, n, me)
    row = lax.broadcasted_iota(jnp.int32, (width, rows_dev), 1)
    pick[...] = jnp.where(row == target, 1.0, 0.0).astype(jnp.bfloat16)
    ends = jnp.where(z > 0, 1, 0) + jnp.where(z < wide_count - 1, 1, 0)
    pl.semaphore_wait(barrier, bits + ends)

    def rows_of(side, i):
        return pl.ds(pl.multiple_of((side * CHUNKS + i) * chunk, chunk), chunk)

    def chain_copy(i, src):
        part = rows_of(core, i)
        return remote(src.at[part, :], top.at[part, :], chain_sems, i, (z, chain_to))

    def near_copy(i, src):
        part = rows_of(core, i)
        return remote(src.at[part, :], top.at[part, :], near_sems, i, (z, mate))

    def seed_copy(i):
        part = rows_of(1, i)
        return pltpu.make_async_remote_copy(
            src_ref=matrix.at[part, :],
            dst_ref=top.at[part, :],
            send_sem=near_sems.at[2, i],
            recv_sem=chain_sems.at[1, i],
            device_id=(z, mate),
            device_id_type=MESH,
        )

    parts = rows_dev // width

    def panel_rows(i):
        return pl.ds(i * width, width)

    def panel_copy(i, src):
        return remote(
            src, panel.at[panel_rows(i), :], panel_sems, i, (z + 1, me)
        )

    own_panel = pltpu.make_async_copy(matrix.at[:, pl.ds(0, width)], panel, local_sem.at[0])
    own_top = pltpu.make_async_copy(matrix.at[pl.ds(0, width), :], top, local_sem.at[1])
    own_lower = pltpu.make_async_copy(
        matrix.at[pl.ds(0, width), pl.ds(0, width)], lower, local_sem.at[2]
    )
    sent_lower = pltpu.make_async_copy(panel.at[panel_rows(0), :], lower, local_sem.at[2])

    @pl.when(z == 0)
    def _():
        for i in range(parts):
            panel_copy(i, matrix.at[panel_rows(i), pl.ds(0, width)]).start()
        own_panel.start()

        @pl.when(root)
        def _():
            own_lower.start()

    @pl.when(root)
    def _():
        for i in range(CHUNKS):
            seed_copy(i).start()
            chain_copy(i, matrix).start()
        for i in range(CHUNKS):
            near_copy(i, matrix).start()
        own_top.start()

    def picked(j):
        load(j).wait()
        rows = jnp.dot(pick[...], slices[j], preferred_element_type=jnp.float32)
        return rows.astype(jnp.bfloat16)

    def pair_copy(r):
        return remote(outgoing.at[r], arrived.at[r], pair_sems, r, (z, mate))

    def for_mate(i, carry):
        r = half - 1 - i
        outgoing[r] = picked(slice_of(r, 1 - core))
        pair_copy(r).start()
        return carry

    lax.fori_loop(0, half, for_mate, 0)

    def for_me(i, carry):
        r = half - 1 - i
        held[r] = picked(slice_of(r, core))
        return carry

    lax.fori_loop(0, half, for_me, 0)

    def forward_chunk(i):
        @pl.when(jnp.logical_not(root))
        def _():
            chain_copy(i, top).wait_recv()

            @pl.when(has_next)
            def _():
                chain_copy(i, top).start()

            @pl.when(chip > 0)
            def _():
                near_copy(i, top).start()

    def forward_panel(i):
        @pl.when(z > 0)
        def _():
            panel_copy(i, panel.at[panel_rows(i), :]).wait_recv()

            @pl.when(z < wide_count - 1)
            def _():
                panel_copy(i, panel.at[panel_rows(i), :]).start()

    def halve_copy(k, r):
        keep = r - 2 ** (bits - 2 - k)
        return remote(
            held.at[r], partial.at[2 ** (bits - 2 - k) - 1 + keep], halve_sems, r, (z, partner(k))
        )

    def halve_arrived(k, r):
        at = 2 ** (bits - 2 - k)
        return remote(held.at[r], partial.at[at - 1 + r], halve_sems, at + r, (z, partner(k)))

    def pair_step(i, carry):
        r = half - 1 - i
        pair_copy(r).wait_recv()
        held[r] = held[r] + arrived[r]
        return carry

    def first_send(i, carry):
        pair_step(i, carry)
        halve_copy(0, half - 1 - i).start()
        return carry

    for i in range(2):
        forward_chunk(i)
    quarter = half // 2
    lax.fori_loop(0, quarter, first_send, 0)
    lax.fori_loop(quarter, half, pair_step, 0)
    for i in range(2, 4):
        forward_chunk(i)
    forward_panel(0)

    def lower_copy(q):
        return pltpu.make_async_remote_copy(
            src_ref=lower,
            dst_ref=lower,
            send_sem=lower_sems.at[q],
            recv_sem=lower_sems.at[bits],
            device_id=(z, flip[q]),
            device_id_type=MESH,
        )

    @pl.when(root)
    def _():
        @pl.when(z > 0)
        def _():
            sent_lower.start()

        sent_lower.wait()

    @pl.when(jnp.logical_not(root))
    def _():
        lower_copy(0).wait_recv()

    for q in range(1, bits):

        @pl.when((core == 0) & (me < 2**q))
        def _():
            lower_copy(q).start()

    @pl.when(core == 0)
    def _():
        lower_copy(0).start()

    for k in range(bits - 2):
        at = 2 ** (bits - 2 - k)
        for r in range(at - 1, -1, -1):
            halve_arrived(k, r).wait_recv()
            held[r] = held[r] + partial[at - 1 + r]
            if r >= at // 2:
                halve_copy(k + 1, r).start()

    r0 = lax.broadcasted_iota(jnp.int32, (width, width), 0)
    c0 = lax.broadcasted_iota(jnp.int32, (width, width), 1)
    apart = jnp.bitwise_xor(r0, c0)
    strict = jnp.where(r0 > c0, lower[...].astype(jnp.float32), 0.0)
    inverse[...] = jnp.where(r0 == c0, 1.0, 0.0) - jnp.where(apart == 1, strict, 0.0)

    def double_block(size):
        between = jnp.where((apart >= size) & (apart < 2 * size), strict, 0.0)
        now = inverse[...]
        left = jnp.dot(
            now, between, precision=lax.Precision.HIGHEST, preferred_element_type=jnp.float32
        )
        inverse[...] = now - jnp.dot(
            left, now, precision=lax.Precision.HIGHEST, preferred_element_type=jnp.float32
        )

    sizes = [2**level for level in range(1, width.bit_length() - 1)]
    for i in range(4, CHUNKS):
        forward_chunk(i)
        for size in sizes[:2]:
            double_block(size)
        sizes = sizes[2:]
    for size in sizes:
        double_block(size)
    for i in range(1, parts):
        forward_panel(i)

    halve_arrived(bits - 2, 0).wait_recv()
    rows = held[0] + partial[0]
    whole = inverse[...]
    high = whole.astype(jnp.bfloat16)
    rest = (whole - high.astype(jnp.float32)).astype(jnp.bfloat16)
    solved[...] = (
        jnp.dot(high, rows, preferred_element_type=jnp.float32)
        + jnp.dot(rest, rows, preferred_element_type=jnp.float32)
    ).astype(jnp.bfloat16)

    def gather_copy(k, r, src):
        at = 2 ** (bits - 2 - k)
        j = slice_of(r, core)
        return remote(src, upper.at[j], gather_sems, at + r, (z, partner(k)))

    def gather_arrived(k, r):
        at = 2 ** (bits - 2 - k)
        j = slice_of(at + r, core)
        return remote(upper.at[j], upper.at[j], gather_sems, at + r, (z, partner(k)))

    def share_copy(r, src):
        return remote(src, upper.at[slice_of(r, core)], share_sems, r, (z, mate))

    def share_arrived(r):
        j = slice_of(r, 1 - core)
        return remote(upper.at[j], upper.at[j], share_sems, r, (z, mate))

    own_upper = pltpu.make_async_copy(solved, upper.at[me], local_sem.at[3])
    for k in range(bits - 2, -1, -1):
        gather_copy(k, 0, solved).start()
    share_copy(0, solved).start()
    own_upper.start()
    for k in range(bits - 2, -1, -1):
        at = 2 ** (bits - 2 - k)
        for r in range(at):
            gather_arrived(k, r).wait_recv()
            here = upper.at[slice_of(at + r, core)]
            for lesser in range(k - 1, -1, -1):
                gather_copy(lesser, at + r, here).start()
            share_copy(at + r, here).start()
    for r in range(half):
        share_arrived(r).wait_recv()

    for r in range(half):
        pair_copy(r).wait_send()
        share_copy(r, solved).wait_send()
    for k in range(bits - 1):
        at = 2 ** (bits - 2 - k)
        for r in range(at):
            halve_copy(k, at + r).wait_send()
            gather_copy(k, r, solved).wait_send()
    own_upper.wait()

    @pl.when(z == 0)
    def _():
        own_panel.wait()

    @pl.when(z < wide_count - 1)
    def _():
        for i in range(parts):
            panel_copy(i, panel.at[panel_rows(i), :]).wait_send()

    for q in range(1, bits):

        @pl.when((core == 0) & (me < 2**q))
        def _():
            lower_copy(q).wait_send()

    @pl.when(core == 0)
    def _():
        lower_copy(0).wait_send()

    @pl.when(root)
    def _():
        own_top.wait()
        for i in range(CHUNKS):
            seed_copy(i).wait_send()

    @pl.when(has_next)
    def _():
        for i in range(CHUNKS):
            chain_copy(i, top).wait_send()

    @pl.when((chip > 0) | (core == 0))
    def _():
        for i in range(CHUNKS):
            near_copy(i, top).wait_send()

    def mate_rows(i):
        part = rows_of(1 - core, i)
        return remote(top.at[part, :], top.at[part, :], near_sems, i, (z, mate))

    @pl.when(jnp.logical_not(root))
    def _():
        for i in range(CHUNKS):
            mate_rows(i).wait_recv()


def update(narrow_count, place, pivots, matrix, panel, top, upper, out, factors, kept):
    rows_dev, width = panel.shape
    narrow_pos = place[0]
    wide_pos = place[1]

    @pl.when(pl.program_id(0) == 0)
    def _():
        target = local_targets(pivots[...], width, narrow_count, narrow_pos)
        row = lax.broadcasted_iota(jnp.int32, (rows_dev, width), 0)
        hit = jnp.where(row == target, 1.0, 0.0)
        factors[:, :width] = hit.astype(jnp.bfloat16)
        factors[:, width:] = -panel[...]
        kept[...] = jnp.broadcast_to(1.0 - jnp.sum(hit, axis=1, keepdims=True), kept.shape)

    solved = upper[0]
    terms = jnp.concatenate([top[...], solved], axis=0)
    change = jnp.dot(factors[...], terms, preferred_element_type=jnp.float32)
    stay = kept[:, :1] > 0.5
    base = jnp.where(stay, matrix[...].astype(jnp.float32), 0.0)
    out[...] = (base + change).astype(jnp.bfloat16)

    @pl.when(narrow_pos == 0)
    def _():
        out[:width, :] = solved

    cut = matrix.shape[1]

    @pl.when((wide_pos == 0) & (pl.program_id(0) * cut < width))
    def _():
        own = min(cut, width)
        out[:, :own] = matrix[:, :own]


def shards(matrix, pivots):
    rows_dev, cols = matrix.shape
    width = pivots.shape[0]
    n = lax.axis_size("narrow")
    wide_count = lax.axis_size("wide")
    half = n // 2
    cut = cols // n
    bits = n.bit_length() - 1
    bf16 = jnp.bfloat16
    anywhere = pl.BlockSpec(memory_space=pl.ANY)
    dma = pltpu.SemaphoreType.DMA
    upper, top, panel = pl.pallas_call(
        functools.partial(exchange, n, wide_count),
        out_shape=(
            jax.ShapeDtypeStruct((n, width, cut), bf16),
            jax.ShapeDtypeStruct((width, cols), bf16),
            jax.ShapeDtypeStruct((rows_dev, width), bf16),
        ),
        in_specs=[pl.BlockSpec(memory_space=pltpu.VMEM), anywhere],
        out_specs=(anywhere, anywhere, anywhere),
        scratch_shapes=[
            pltpu.VMEM((n, rows_dev, cut), bf16),
            pltpu.VMEM((width, rows_dev), bf16),
            pltpu.VMEM((half, width, cut), bf16),
            pltpu.VMEM((half, width, cut), bf16),
            pltpu.VMEM((half, width, cut), bf16),
            pltpu.VMEM((half, width, cut), bf16),
            pltpu.VMEM((width, width), bf16),
            pltpu.VMEM((width, width), jnp.float32),
            pltpu.VMEM((width, cut), bf16),
            dma((n,)),
            dma((4,)),
            dma((2, half)),
            dma((2, half)),
            dma((2, half)),
            dma((2, half)),
            dma((2, CHUNKS)),
            dma((3, CHUNKS)),
            dma((2, rows_dev // width)),
            dma((bits + 1,)),
        ],
        compiler_params=pltpu.CompilerParams(
            collective_id=0, has_side_effects=True, vmem_limit_bytes=40 * 2**20
        ),
        cost_estimate=pl.CostEstimate(
            flops=2 * width * rows_dev * cols, bytes_accessed=4 * rows_dev * cols, transcendentals=0
        ),
        name="exchange",
    )(pivots.reshape(width, 1), matrix)
    place = jnp.stack([lax.axis_index("narrow"), lax.axis_index("wide")]).astype(jnp.int32)
    return pl.pallas_call(
        functools.partial(update, n),
        out_shape=jax.ShapeDtypeStruct((rows_dev, cols), bf16),
        grid=(n,),
        in_specs=[
            pl.BlockSpec(memory_space=pltpu.SMEM),
            pl.BlockSpec((1, width), lambda j: (0, 0)),
            pl.BlockSpec((rows_dev, cut), lambda j: (0, j)),
            pl.BlockSpec((rows_dev, width), lambda j: (0, 0)),
            pl.BlockSpec((width, cut), lambda j: (0, j)),
            pl.BlockSpec((1, width, cut), lambda j: (j, 0, 0)),
        ],
        out_specs=pl.BlockSpec((rows_dev, cut), lambda j: (0, j)),
        scratch_shapes=[
            pltpu.VMEM((rows_dev, 2 * width), bf16),
            pltpu.VMEM((rows_dev, 128), jnp.float32),
        ],
        compiler_params=pltpu.CompilerParams(vmem_limit_bytes=40 * 2**20),
        cost_estimate=pl.CostEstimate(
            flops=4 * width * rows_dev * cols, bytes_accessed=5 * rows_dev * cols, transcendentals=0
        ),
        name="update",
    )(place, pivots.reshape(1, width), matrix, panel, top, upper)


def solution(mesh):
    placed = (P("narrow", "wide"), P())
    return jax.shard_map(
        shards, mesh=mesh, in_specs=placed, out_specs=P("narrow", "wide"), check_vma=False
    )
```

```python
import functools

import jax
import jax.numpy as jnp
from jax import lax
from jax.experimental import pallas as pl
from jax.experimental.pallas import tpu as pltpu
from jax.sharding import PartitionSpec as P

MESH = pl.DeviceIdType.MESH
CHUNKS = 8


def local_targets(pivots, width, narrow_count, narrow_pos):
    blocks = jnp.right_shift(pivots, width.bit_length() - 1)
    owner = jnp.bitwise_and(blocks, narrow_count - 1)
    inner = jnp.right_shift(blocks, narrow_count.bit_length() - 1)
    rows = inner * width + jnp.bitwise_and(pivots, width - 1)
    return jnp.where(owner == narrow_pos, rows, -1)


def exchange(
    narrow_count,
    wide_count,
    pivots,
    matrix,
    upper,
    swapped,
    panel,
    top,
    slices,
    hits,
    kept,
    pick,
    outgoing,
    held,
    arrived,
    partial,
    lower,
    inverse,
    solved,
    load_sem,
    local_sem,
    pair_sems,
    halve_sems,
    gather_sems,
    share_sems,
    chain_sems,
    near_sems,
    panel_sems,
    lower_sems,
    across_sems,
):
    n = narrow_count
    bits = n.bit_length() - 1
    half = n // 2
    chips = half
    rows_dev, cols = matrix.shape
    width = pick.shape[0]
    cut = cols // n
    z = lax.axis_index("wide")
    me = lax.axis_index("narrow")
    core = me % 2
    chip = me // 2
    mate = me + 1 - 2 * core
    value = [(me // 2**q) % 2 for q in range(bits)]
    flip = [me + (1 - 2 * value[q]) * 2**q for q in range(bits)]

    def by_core(side, first, second):
        return first * (1 - side) + second * side

    def slice_of(r, side):
        total = side
        for q in range(1, bits):
            f0 = (r // 2 ** (bits - 1 - q)) % 2
            f1 = (r // 2 ** (q - 1)) % 2
            f = by_core(side, f0, f1)
            total = total + (value[q] + f * (1 - 2 * value[q])) * 2**q
        return total

    def partner(k):
        return by_core(core, flip[1 + k], flip[bits - 1 - k])

    def remote(src, dst, sems, i, to):
        return pltpu.make_async_remote_copy(
            src_ref=src,
            dst_ref=dst,
            send_sem=sems.at[0, i],
            recv_sem=sems.at[1, i],
            device_id=to,
            device_id_type=MESH,
        )

    ring = 0
    for q in range(1, bits):
        ring = ring + (sum(value[q:]) % 2) * 2 ** (q - 1)
    order = by_core(core, ring, (chips - ring) % chips)
    following = (ring + 1 - 2 * core + chips) % chips
    chip_next = 0
    for q in range(bits - 1):
        low = (following // 2**q) % 2
        high = (following // 2 ** (q + 1)) % 2
        chip_next = chip_next + ((low + high) % 2) * 2**q
    chain_to = chip_next * 2 + core
    chunk = width // 2 // CHUNKS
    root = me == 0
    has_next = order < chips - 1

    def load(j):
        return pltpu.make_async_copy(
            matrix.at[:, pl.ds(pl.multiple_of(j * cut, cut), cut)],
            slices.at[j],
            load_sem.at[j],
        )

    for j in range(n):
        load(j).start()

    barrier = pltpu.get_barrier_semaphore()
    for q in range(bits):
        pl.semaphore_signal(barrier, inc=1, device_id=(z, flip[q]), device_id_type=MESH)

    @pl.when(z > 0)
    def _():
        pl.semaphore_signal(barrier, inc=1, device_id=(0, me), device_id_type=MESH)

    target = local_targets(pivots[...], width, n, me)
    row = lax.broadcasted_iota(jnp.int32, (rows_dev, width), 0)
    hit = jnp.where(row == target, 1.0, 0.0)
    hits[...] = hit.astype(jnp.bfloat16)
    pick[...] = jnp.transpose(hit).astype(jnp.bfloat16)
    kept[...] = jnp.broadcast_to(1.0 - jnp.sum(hit, axis=1, keepdims=True), kept.shape)
    pl.semaphore_wait(barrier, bits + jnp.where(z == 0, wide_count - 1, 0))

    def rows_of(side, i):
        return pl.ds(pl.multiple_of((side * CHUNKS + i) * chunk, chunk), chunk)

    def chain_copy(i, src):
        part = rows_of(core, i)
        return remote(src.at[part, :], top.at[part, :], chain_sems, i, (z, chain_to))

    def near_copy(i, src):
        part = rows_of(core, i)
        return remote(src.at[part, :], top.at[part, :], near_sems, i, (z, mate))

    def seed_copy(i):
        part = rows_of(1, i)
        return pltpu.make_async_remote_copy(
            src_ref=matrix.at[part, :],
            dst_ref=top.at[part, :],
            send_sem=near_sems.at[2, i],
            recv_sem=chain_sems.at[1, i],
            device_id=(z, mate),
            device_id_type=MESH,
        )

    def panel_copy(to):
        return pltpu.make_async_remote_copy(
            src_ref=matrix.at[:, pl.ds(0, width)],
            dst_ref=panel,
            send_sem=panel_sems.at[to],
            recv_sem=panel_sems.at[0],
            device_id=(to, me),
            device_id_type=MESH,
        )

    def lower_across(to):
        return pltpu.make_async_remote_copy(
            src_ref=matrix.at[pl.ds(0, width), pl.ds(0, width)],
            dst_ref=lower,
            send_sem=across_sems.at[to],
            recv_sem=across_sems.at[0],
            device_id=(to, me),
            device_id_type=MESH,
        )

    own_panel = pltpu.make_async_copy(matrix.at[:, pl.ds(0, width)], panel, local_sem.at[0])
    own_top = pltpu.make_async_copy(matrix.at[pl.ds(0, width), :], top, local_sem.at[1])
    own_lower = pltpu.make_async_copy(
        matrix.at[pl.ds(0, width), pl.ds(0, width)], lower, local_sem.at[2]
    )

    @pl.when((z == 0) & root)
    def _():
        for to in range(wide_count - 1, 0, -1):
            lower_across(to).start()
        own_lower.start()

    @pl.when(root)
    def _():
        for i in range(CHUNKS):
            seed_copy(i).start()
            chain_copy(i, matrix).start()
        for i in range(CHUNKS):
            near_copy(i, matrix).start()
        own_top.start()

    def picked(j):
        load(j).wait()
        rows = jnp.dot(pick[...], slices[j], preferred_element_type=jnp.float32)
        return rows.astype(jnp.bfloat16)

    def pair_copy(r):
        return remote(outgoing.at[r], arrived.at[r], pair_sems, r, (z, mate))

    def for_mate(i, carry):
        r = half - 1 - i
        outgoing[r] = picked(slice_of(r, 1 - core))
        pair_copy(r).start()
        return carry

    lax.fori_loop(0, half, for_mate, 0)

    def for_me(i, carry):
        r = half - 1 - i
        held[r] = picked(slice_of(r, core))
        return carry

    lax.fori_loop(0, half, for_me, 0)

    def forward_chunk(i):
        @pl.when(jnp.logical_not(root))
        def _():
            chain_copy(i, top).wait_recv()

            @pl.when(has_next)
            def _():
                chain_copy(i, top).start()

            @pl.when(chip > 0)
            def _():
                near_copy(i, top).start()

    def halve_copy(k, r):
        keep = r - 2 ** (bits - 2 - k)
        return remote(
            held.at[r], partial.at[2 ** (bits - 2 - k) - 1 + keep], halve_sems, r, (z, partner(k))
        )

    def halve_arrived(k, r):
        at = 2 ** (bits - 2 - k)
        return remote(held.at[r], partial.at[at - 1 + r], halve_sems, at + r, (z, partner(k)))

    def pair_step(i, carry):
        r = half - 1 - i
        pair_copy(r).wait_recv()
        held[r] = held[r] + arrived[r]
        return carry

    def first_send(i, carry):
        pair_step(i, carry)
        halve_copy(0, half - 1 - i).start()
        return carry

    @pl.when(z == 0)
    def _():
        for to in range(wide_count - 1, 0, -1):
            panel_copy(to).start()
        own_panel.start()

    for i in range(CHUNKS):
        forward_chunk(i)
    quarter = half // 2
    lax.fori_loop(0, quarter, first_send, 0)
    lax.fori_loop(quarter, half, pair_step, 0)

    def lower_copy(q):
        return pltpu.make_async_remote_copy(
            src_ref=lower,
            dst_ref=lower,
            send_sem=lower_sems.at[q],
            recv_sem=lower_sems.at[bits],
            device_id=(z, flip[q]),
            device_id_type=MESH,
        )

    @pl.when(root)
    def _():
        @pl.when(z > 0)
        def _():
            lower_across(0).wait_recv()

        @pl.when(z == 0)
        def _():
            own_lower.wait()

    @pl.when(jnp.logical_not(root))
    def _():
        lower_copy(0).wait_recv()

    for q in range(1, bits):

        @pl.when((core == 0) & (me < 2**q))
        def _():
            lower_copy(q).start()

    @pl.when(core == 0)
    def _():
        lower_copy(0).start()

    def mate_rows(i):
        part = rows_of(1 - core, i)
        return remote(top.at[part, :], top.at[part, :], near_sems, i, (z, mate))

    @pl.when(root)
    def _():
        own_top.wait()

    @pl.when(jnp.logical_not(root))
    def _():
        for i in range(CHUNKS):
            mate_rows(i).wait_recv()

    def store(j):
        part = pl.ds(pl.multiple_of(j * cut, cut), cut)
        return pltpu.make_async_copy(slices.at[j], swapped.at[:, part], load_sem.at[j])

    def swap(j, carry):
        part = pl.ds(pl.multiple_of(j * cut, cut), cut)
        moved = jnp.dot(hits[...], top[:, part], preferred_element_type=jnp.float32)
        stays = kept[:, :1] > 0.5
        base = jnp.where(stays, slices[j].astype(jnp.float32), 0.0)
        slices[j] = (base + moved).astype(jnp.bfloat16)
        store(j).start()
        return carry

    lax.fori_loop(0, half, swap, 0)

    for k in range(bits - 2):
        at = 2 ** (bits - 2 - k)
        for r in range(at - 1, -1, -1):
            halve_arrived(k, r).wait_recv()
            held[r] = held[r] + partial[at - 1 + r]
            if r >= at // 2:
                halve_copy(k + 1, r).start()

    r0 = lax.broadcasted_iota(jnp.int32, (width, width), 0)
    c0 = lax.broadcasted_iota(jnp.int32, (width, width), 1)
    apart = jnp.bitwise_xor(r0, c0)
    strict = jnp.where(r0 > c0, lower[...].astype(jnp.float32), 0.0)
    inverse[...] = jnp.where(r0 == c0, 1.0, 0.0) - jnp.where(apart == 1, strict, 0.0)

    def split(x):
        high = x.astype(jnp.bfloat16)
        return high, (x - high.astype(jnp.float32)).astype(jnp.bfloat16)

    def dot(a, b):
        return jnp.dot(a, b, preferred_element_type=jnp.float32)

    def double_block(size):
        inside = (apart >= size) & (apart < 2 * size)
        between = jnp.where(inside, strict, 0.0).astype(jnp.bfloat16)
        now = inverse[...]
        high, rest = split(now)
        left_high, left_rest = split(dot(high, between) + dot(rest, between))
        inverse[...] = now - (
            dot(left_high, high) + (dot(left_high, rest) + dot(left_rest, high))
        )

    sizes = [2**level for level in range(1, width.bit_length() - 1)]
    for size in sizes:
        double_block(size)

    lax.fori_loop(half, n, swap, 0)
    halve_arrived(bits - 2, 0).wait_recv()
    rows = held[0] + partial[0]
    high, rest = split(inverse[...])
    solved[...] = (dot(high, rows) + dot(rest, rows)).astype(jnp.bfloat16)

    def gather_copy(k, r, src):
        at = 2 ** (bits - 2 - k)
        j = slice_of(r, core)
        return remote(src, upper.at[j], gather_sems, at + r, (z, partner(k)))

    def gather_arrived(k, r):
        at = 2 ** (bits - 2 - k)
        j = slice_of(at + r, core)
        return remote(upper.at[j], upper.at[j], gather_sems, at + r, (z, partner(k)))

    def share_copy(r, src):
        return remote(src, upper.at[slice_of(r, core)], share_sems, r, (z, mate))

    def share_arrived(r):
        j = slice_of(r, 1 - core)
        return remote(upper.at[j], upper.at[j], share_sems, r, (z, mate))

    own_upper = pltpu.make_async_copy(solved, upper.at[me], local_sem.at[3])
    for k in range(bits - 2, -1, -1):
        gather_copy(k, 0, solved).start()
    share_copy(0, solved).start()
    own_upper.start()
    for k in range(bits - 2, -1, -1):
        at = 2 ** (bits - 2 - k)
        for r in range(at):
            gather_arrived(k, r).wait_recv()
            here = upper.at[slice_of(at + r, core)]
            for lesser in range(k - 1, -1, -1):
                gather_copy(lesser, at + r, here).start()
            share_copy(at + r, here).start()
    for r in range(half):
        share_arrived(r).wait_recv()

    for r in range(half):
        pair_copy(r).wait_send()
        share_copy(r, solved).wait_send()
    for k in range(bits - 1):
        at = 2 ** (bits - 2 - k)
        for r in range(at):
            halve_copy(k, at + r).wait_send()
            gather_copy(k, r, solved).wait_send()
    own_upper.wait()

    @pl.when(z == 0)
    def _():
        own_panel.wait()
        for to in range(1, wide_count):
            panel_copy(to).wait_send()

        @pl.when(root)
        def _():
            for to in range(1, wide_count):
                lower_across(to).wait_send()

    @pl.when(z > 0)
    def _():
        panel_copy(0).wait_recv()

    for q in range(1, bits):

        @pl.when((core == 0) & (me < 2**q))
        def _():
            lower_copy(q).wait_send()

    @pl.when(core == 0)
    def _():
        lower_copy(0).wait_send()

    @pl.when(root)
    def _():
        for i in range(CHUNKS):
            seed_copy(i).wait_send()

    @pl.when(has_next)
    def _():
        for i in range(CHUNKS):
            chain_copy(i, top).wait_send()

    @pl.when((chip > 0) | (core == 0))
    def _():
        for i in range(CHUNKS):
            near_copy(i, top).wait_send()

    for j in range(n):
        store(j).wait()


def update(place, swapped, panel, upper, out):
    width = panel.shape[1]
    cut = swapped.shape[1]
    step = pl.program_id(0)
    solved = upper[0]
    product = jnp.dot(panel[...], solved, preferred_element_type=jnp.float32)
    out[...] = (swapped[...].astype(jnp.float32) - product).astype(jnp.bfloat16)

    @pl.when(place[0] == 0)
    def _():
        out[:width, :] = solved

    @pl.when((place[1] == 0) & (step * cut < width))
    def _():
        if cut >= width:
            out[:, :width] = panel[...]
        else:
            out[...] = panel[:, pl.ds(pl.multiple_of(step * cut, cut), cut)]


def shards(matrix, pivots):
    rows_dev, cols = matrix.shape
    width = pivots.shape[0]
    n = lax.axis_size("narrow")
    wide_count = lax.axis_size("wide")
    half = n // 2
    cut = cols // n
    bits = n.bit_length() - 1
    bf16 = jnp.bfloat16
    anywhere = pl.BlockSpec(memory_space=pl.ANY)
    dma = pltpu.SemaphoreType.DMA
    upper, swapped, panel = pl.pallas_call(
        functools.partial(exchange, n, wide_count),
        out_shape=(
            jax.ShapeDtypeStruct((n, width, cut), bf16),
            jax.ShapeDtypeStruct((rows_dev, cols), bf16),
            jax.ShapeDtypeStruct((rows_dev, width), bf16),
        ),
        in_specs=[pl.BlockSpec(memory_space=pltpu.VMEM), anywhere],
        out_specs=(anywhere, anywhere, anywhere),
        scratch_shapes=[
            pltpu.VMEM((width, cols), bf16),
            pltpu.VMEM((n, rows_dev, cut), bf16),
            pltpu.VMEM((rows_dev, width), bf16),
            pltpu.VMEM((rows_dev, 128), jnp.float32),
            pltpu.VMEM((width, rows_dev), bf16),
            pltpu.VMEM((half, width, cut), bf16),
            pltpu.VMEM((half, width, cut), bf16),
            pltpu.VMEM((half, width, cut), bf16),
            pltpu.VMEM((half, width, cut), bf16),
            pltpu.VMEM((width, width), bf16),
            pltpu.VMEM((width, width), jnp.float32),
            pltpu.VMEM((width, cut), bf16),
            dma((n,)),
            dma((4,)),
            dma((2, half)),
            dma((2, half)),
            dma((2, half)),
            dma((2, half)),
            dma((2, CHUNKS)),
            dma((3, CHUNKS)),
            dma((wide_count,)),
            dma((bits + 1,)),
            dma((wide_count,)),
        ],
        compiler_params=pltpu.CompilerParams(
            collective_id=0, has_side_effects=True, vmem_limit_bytes=40 * 2**20
        ),
        cost_estimate=pl.CostEstimate(
            flops=2 * width * rows_dev * cols, bytes_accessed=4 * rows_dev * cols, transcendentals=0
        ),
        name="exchange",
    )(pivots.reshape(1, width), matrix)
    place = jnp.stack([lax.axis_index("narrow"), lax.axis_index("wide")]).astype(jnp.int32)
    return pl.pallas_call(
        update,
        out_shape=jax.ShapeDtypeStruct((rows_dev, cols), bf16),
        grid=(n,),
        in_specs=[
            pl.BlockSpec(memory_space=pltpu.SMEM),
            pl.BlockSpec((rows_dev, cut), lambda j: (0, j)),
            pl.BlockSpec((rows_dev, width), lambda j: (0, 0)),
            pl.BlockSpec((1, width, cut), lambda j: (j, 0, 0)),
        ],
        out_specs=pl.BlockSpec((rows_dev, cut), lambda j: (0, j)),
        compiler_params=pltpu.CompilerParams(vmem_limit_bytes=40 * 2**20),
        cost_estimate=pl.CostEstimate(
            flops=2 * width * rows_dev * cols, bytes_accessed=5 * rows_dev * cols, transcendentals=0
        ),
        name="update",
    )(place, swapped, panel, upper)


def solution(mesh):
    placed = (P("narrow", "wide"), P())
    return jax.shard_map(
        shards, mesh=mesh, in_specs=placed, out_specs=P("narrow", "wide"), check_vma=False
    )
```
